128 devices in a mesh: row: 8 (over y, core), col: 16 (over x, z).
Axes of the slice: x: 4, y: 4, z: 4, core: 2. Of those that a mesh axis runs over, the one named last changes fastest.
Arguments:
- transition: bfloat16 [12288, 12288], P('row', 'col'), may hold values from 0 to 36.084392, as said below
- tile_pattern: int32 [96, 96], P('row', 'col'), may hold values from 0 to 1, as said below
- kept_tiles: int32 [96, 48], P('row', 'col'), may hold values from 0 to 1, as said below
Outputs:
- next_panel: float32 [12288, 6144], P('row', 'col')
- chaos: float32 [], replicated
The draws below stay inside these ranges and needn't reach their ends.
Inputs may be any that keep to these rules, and one draw needn't show every extreme that they name: `tile_pattern`: each device's block of 12 x 6 tiles holds at most 36 nonzero tiles, and some block holds exactly 36. Every diagonal tile is nonzero. `kept_tiles`: for panel tile column p, the tile in tile row (p // 3) * 6 + p % 3 is always kept. `transition`: all entries are positive.
All inputs are finite; a program needn't handle non-finite values.
Results may differ from the reference program's by a relative error of at most 0.0003.
Values may be sent and summed in bfloat16 or wider, within the bound.
A program may use at most 128 MiB of HBM per device.

```python
import math
import jax
import jax.numpy as jnp

TILE = 128
RT = 12
PT = 3
NT = 96
KT = 6
KDEV = 36
NODES = 12288
PANEL = 6144
N_COL = 16


def draw_transition(key, part):
    key_base, key_rows, key_cols = jax.random.split(key, 3)
    positions = jnp.arange(NODES).astype(jnp.float32) / (NODES - 1)
    base = jnp.exp(jax.random.uniform(key_base, (NODES, NODES), jnp.float32, math.log(0.2), math.log(5.0)))
    row_scale = jnp.exp(jax.random.uniform(key_rows, (NODES, 1), jnp.float32, 0.0, math.log(10.0)))
    col_scale = jnp.exp(jax.random.uniform(key_cols, (1, NODES), jnp.float32, 0.0, math.log(10.0)))
    ramp = 1.0 + 2.0 * positions
    values = base * row_scale * col_scale * ramp[:, None] * float(NODES) ** (-0.5)
    return values.astype(jnp.bfloat16)


def draw_tile_pattern(key, part):
    key_level, key_force, key_order = jax.random.split(key, 3)
    block_rows = NT // RT
    block_cols = NT // KT
    levels = jax.random.randint(key_level, (block_rows, block_cols), 0, 4).astype(jnp.int32)
    forced = jax.random.randint(key_force, (), 0, block_rows * block_cols).astype(jnp.int32)
    block_ids = jnp.arange(block_rows * block_cols).astype(jnp.int32).reshape(block_rows, block_cols)
    levels = jnp.where(block_ids == forced, 0, levels)
    targets = jnp.right_shift(jnp.full((block_rows, block_cols), KDEV, jnp.int32), levels)
    row_ids = jnp.arange(NT).astype(jnp.int32)[:, None]
    col_ids = jnp.arange(NT).astype(jnp.int32)[None, :]
    diagonal = (row_ids == col_ids).astype(jnp.int32)
    scores = jax.random.permutation(key_order, NT * NT).astype(jnp.int32).reshape(NT, NT) + diagonal * (NT * NT)
    grouped = scores.reshape(block_rows, RT, block_cols, KT).transpose(0, 2, 1, 3).reshape(block_rows, block_cols, RT * KT)
    diag_grouped = diagonal.reshape(block_rows, RT, block_cols, KT).transpose(0, 2, 1, 3).reshape(block_rows, block_cols, RT * KT)
    ranks = jnp.sum((grouped[..., None, :] > grouped[..., :, None]).astype(jnp.int32), axis=-1)
    needed = jnp.maximum(jnp.maximum(targets, jnp.sum(diag_grouped, axis=-1)), 1)
    chosen = (ranks < needed[..., None]).astype(jnp.int32)
    return chosen.reshape(block_rows, block_cols, RT, KT).transpose(0, 2, 1, 3).reshape(NT, NT)


def draw_kept_tiles(key, part):
    panel_tiles = PT * N_COL
    kept = (jax.random.randint(key, (NT, panel_tiles), 0, 4) > 0).astype(jnp.int32)
    col_ids = jnp.arange(panel_tiles).astype(jnp.int32)
    home_rows = col_ids // PT * KT + col_ids % PT
    row_ids = jnp.arange(NT).astype(jnp.int32)[:, None]
    return jnp.where(row_ids == home_rows[None, :], 1, kept).astype(jnp.int32)


def setup_inputs(seed: int = 0) -> dict:
    splits = jax.random.split(jax.random.key(seed), 4)
    return {
        "transition": draw_transition(jax.random.fold_in(splits[3], 71), 0),
        "tile_pattern": draw_tile_pattern(jax.random.fold_in(splits[3], 71), 0),
        "kept_tiles": draw_kept_tiles(jax.random.fold_in(splits[3], 71), 0),
    }


def expand_tiles(tile_mask):
    return jnp.repeat(jnp.repeat(tile_mask, TILE, axis=0), TILE, axis=1)


def reference(transition, tile_pattern, kept_tiles):
    masked = transition * expand_tiles(tile_pattern).astype(jnp.bfloat16)
    column_panel = masked.reshape(NODES, N_COL, KT * TILE)[:, :, :PT * TILE].reshape(NODES, PANEL)
    product = jnp.dot(masked, column_panel, preferred_element_type=jnp.float32)
    pruned = product * expand_tiles(kept_tiles).astype(jnp.float32)
    inflated = pruned * pruned
    col_sums = jnp.sum(inflated, axis=0)
    squares = jnp.sum(inflated * inflated, axis=0)
    normalized = inflated / col_sums
    spread = squares / (col_sums * col_sums)
    chaos_value = jnp.max(jnp.max(normalized, axis=0) - spread)
    return normalized * NODES, chaos_value * NODES
```

```python
import jax
import jax.numpy as jnp
from jax import lax
from jax.experimental import pallas as pl
from jax.experimental.pallas import tpu as pltpu
from jax.sharding import PartitionSpec as P

MESH = pl.DeviceIdType.MESH
T = 128
RT, KT, PT = 12, 6, 3
SLOTS = 36
HALF = 18
QUART = 9
ROWS, KW, W = RT * T, KT * T, PT * T
OFFS = [(dx, dz) for dx in range(4) for dz in range(4)]


def index_kernel(pat_ref, pos_ref, map_ref):
    def clear(s, carry):
        pos_ref[0, s] = 0
        return carry

    lax.fori_loop(0, T, clear, 0)

    def step(p, count):
        v = pat_ref[p % RT, p // RT]
        pos_ref[0, count] = p
        map_ref[0, p] = jnp.where(v > 0, count, SLOTS)
        return count + jnp.where(v > 0, 1, 0)

    lax.fori_loop(0, RT * KT, step, jnp.int32(0))


def main_kernel(pos_ref, kept_ref, map_ref, a_ref, inf_ref, stat_ref, chaos_ref, *scratch):
    bufs = dict(zip(OFFS, scratch[:16]))
    (tiles, ball, acc, dense, meta, meta_s, stats, peaks,
     loc_sem, asem_s, asem_r, bsem_s, bsem_r, msem_s, msem_r, ssem_s, ssem_r, csem_s, csem_r) = scratch[16:]
    row, col = lax.axis_index("row"), lax.axis_index("col")
    y, core = row // 2, row % 2
    x, z = col // 4, col % 4

    def plane(dx, dz):
        return (row, ((x + dx) % 4) * 4 + (z + dz) % 4)

    def line(dy, dc):
        return (((y + dy) % 4) * 2 + (core + dc) % 2, col)

    loads = [
        pltpu.make_async_copy(
            a_ref.at[:, :, pl.ds(c * T, T)], tiles.at[pl.ds(c * RT, RT)], loc_sem.at[c])
        for c in range(KT)
    ]
    for cp in loads:
        cp.start()
    own_meta = pltpu.make_async_copy(map_ref, meta.at[0], loc_sem.at[KT])
    own_meta.start()
    barrier = pltpu.get_barrier_semaphore()
    others = [plane(*o) for o in OFFS[1:]] + [line(dy, dc) for dy in range(4) for dc in range(2) if (dy, dc) != (0, 0)]
    for d in others:
        pl.semaphore_signal(barrier, inc=1, device_id=d, device_id_type=MESH)
    for o in OFFS:
        bufs[o][SLOTS] = jnp.zeros((T, T), jnp.bfloat16)
    own_meta.wait()
    for cp in loads:
        cp.wait()
    own = bufs[(0, 0)]

    def pack(s, carry):
        own[s] = tiles[pos_ref[0, s]]
        return carry

    sends = []

    def remote(src, dst, s_sem, r_sem, dev):
        cp = pltpu.make_async_remote_copy(
            src_ref=src, dst_ref=dst, send_sem=s_sem, recv_sem=r_sem, device_id=dev, device_id_type=MESH)
        cp.start()
        sends.append(cp)
        return cp

    used = {}
    acount = [0]

    def apiece(src_off, axis, sign, lo, n):
        d = [0, 0]
        d[axis] = sign
        dst_off = list(src_off)
        dst_off[axis] = (dst_off[axis] - sign) % 4
        k = acount[0]
        acount[0] += 1
        cp = remote(
            bufs[src_off].at[pl.ds(lo, n)], bufs[tuple(dst_off)].at[pl.ds(lo, n)],
            asem_s.at[k], asem_r.at[k], plane(*d))
        used[(tuple(dst_off), axis, sign, lo)] = cp

    def await_piece(off, axis, sign, lo):
        used[(off, axis, sign, lo)].wait_recv()

    def off(axis, a, b):
        return (a, b) if axis == 0 else (b, a)

    lax.fori_loop(0, SLOTS, pack, 0)
    pl.semaphore_wait(barrier, len(others))

    def spread(h, axis, o):
        apiece(o, axis, 1, h * HALF, HALF)
        apiece(o, axis, -1, h * HALF, HALF)

    def got(h, axis, o1, o3):
        await_piece(o3, axis, 1, h * HALF)
        apiece(o3, axis, 1, h * HALF, QUART)
        await_piece(o1, axis, -1, h * HALF)
        apiece(o1, axis, -1, h * HALF + QUART, QUART)

    def far(h, axis, o2):
        await_piece(o2, axis, 1, h * HALF)
        await_piece(o2, axis, -1, h * HALF + QUART)

    for h in range(2):
        spread(h, h, (0, 0))
    metas = []
    for i, o in enumerate(OFFS[1:]):
        j = OFFS[1:].index(((-o[0]) % 4, (-o[1]) % 4))
        metas.append(remote(meta.at[0], meta.at[1 + j], msem_s.at[i], msem_r.at[j], plane(*o)))
    def own_panel(r, carry):
        for c in range(PT):
            ball[pl.ds(row * ROWS + r * T, T), c * T:(c + 1) * T] = own[meta_s[0, 0, c * RT + r]]
        return carry

    cp = pltpu.make_async_copy(meta.at[0], meta_s.at[0], loc_sem.at[KT])
    cp.start()
    cp.wait()
    lax.fori_loop(0, RT, own_panel, 0)

    def bcopy(k, dy_src, core_src, lo, n, dev):
        blk = ball.at[pl.ds((((y + dy_src) % 4) * 2 + core_src) * ROWS + lo, n)]
        return remote(blk, blk, bsem_s.at[k], bsem_r.at[k], dev)

    HB = ROWS // 2
    b_up = bcopy(0, 0, core, 0, ROWS, line(1, 0))
    b_dn = bcopy(1, 0, core, 0, ROWS, line(-1, 0))
    b_sib = [bcopy(2, 0, core, 0, ROWS, line(0, 1))]
    for h in range(2):
        spread(h, 1 - h, (0, 0))
    for h in range(2):
        got(h, h, off(h, 1, 0), off(h, 3, 0))
    for h in range(2):
        spread(h, 1 - h, off(h, 1, 0))
        spread(h, 1 - h, off(h, 3, 0))
    b_up.wait_recv()
    b_up2 = bcopy(3, 3, core, 0, HB, line(1, 0))
    b_sib.append(bcopy(4, 3, core, 0, ROWS, line(0, 1)))
    b_dn.wait_recv()
    b_dn2 = bcopy(5, 1, core, HB, HB, line(-1, 0))
    b_sib.append(bcopy(6, 1, core, 0, ROWS, line(0, 1)))
    for h in range(2):
        far(h, h, off(h, 2, 0))
    for h in range(2):
        got(h, 1 - h, off(h, 0, 1), off(h, 0, 3))
    for h in range(2):
        spread(h, 1 - h, off(h, 2, 0))
    for cp in metas:
        cp.wait_recv()
    cp = pltpu.make_async_copy(meta.at[pl.ds(1, 15)], meta_s.at[pl.ds(1, 15)], loc_sem.at[KT])
    cp.start()
    cp.wait()
    b_up2.wait_recv()
    b_sib.append(bcopy(7, 2, core, 0, HB, line(0, 1)))
    b_dn2.wait_recv()
    b_sib.append(bcopy(8, 2, core, HB, HB, line(0, 1)))
    for cp in b_sib:
        cp.wait_recv()

    first = [True]

    def multiply(o):
        buf, m = bufs[o], OFFS.index(o)
        zero = first[0]
        first[0] = False
        src = ((x + o[0]) % 4) * 4 + (z + o[1]) % 4

        def expand(r, carry):
            for c in range(KT):
                dense[pl.ds(r * T, T), c * T:(c + 1) * T] = buf[meta_s[m, 0, c * RT + r]]
            return carry

        lax.fori_loop(0, RT, expand, 0)

        def mm(i, carry):
            sl = pl.ds(i * 512, 512)
            p = jnp.dot(dense[sl, :], ball[pl.ds(src * KW, KW), :], preferred_element_type=jnp.float32)
            if zero:
                acc[sl, :] = p
            else:
                acc[sl, :] += p
            return carry

        lax.fori_loop(0, ROWS // 512, mm, 0)

    for o in ((0, 0), (1, 0), (3, 0), (0, 1), (0, 3)):
        multiply(o)
    for s in (1, 3):
        for h in range(2):
            got(h, 1 - h, off(h, s, 1), off(h, s, 3))
    for h in range(2):
        far(h, 1 - h, off(h, 0, 2))
    for o in ((2, 0), (0, 2), (1, 1), (1, 3), (3, 1), (3, 3)):
        multiply(o)
    for h in range(2):
        got(h, 1 - h, off(h, 2, 1), off(h, 2, 3))
    for s in (1, 3):
        for h in range(2):
            far(h, 1 - h, off(h, s, 2))
    for o in ((1, 2), (3, 2), (2, 1), (2, 3)):
        multiply(o)
    for h in range(2):
        far(h, 1 - h, off(h, 2, 2))
    multiply((2, 2))

    sums = [jnp.zeros((8, T), jnp.float32)] * PT
    sqs = [jnp.zeros((8, T), jnp.float32)] * PT
    mxs = [jnp.zeros((8, T), jnp.float32)] * PT

    def finish(r, carry):
        out = []
        for c in range(PT):
            s, q, m = carry[c]
            sl = (pl.ds(r * T, T), slice(c * T, (c + 1) * T))
            v = acc[sl] * kept_ref[r, c].astype(jnp.float32)
            v = v * v
            acc[sl] = v
            v8 = v.reshape(T // 8, 8, T)
            out.append((s + jnp.sum(v8, axis=0), q + jnp.sum(v8 * v8, axis=0), jnp.maximum(m, jnp.max(v8, axis=0))))
        return tuple(out)

    fin = lax.fori_loop(0, RT, finish, tuple((sums[c], sqs[c], mxs[c]) for c in range(PT)))
    out_cp = pltpu.make_async_copy(acc, inf_ref, loc_sem.at[0])
    out_cp.start()
    for c in range(PT):
        s, q, m = fin[c]
        stats[row, 0:1, c * T:(c + 1) * T] = jnp.sum(s, axis=0, keepdims=True)
        stats[row, 1:2, c * T:(c + 1) * T] = jnp.sum(q, axis=0, keepdims=True)
        stats[row, 2:3, c * T:(c + 1) * T] = jnp.max(m, axis=0, keepdims=True)
    lines = [(dy, dc) for dy in range(4) for dc in range(2) if (dy, dc) != (0, 0)]
    cps = []
    for i, (dy, dc) in enumerate(lines):
        j = lines.index(((-dy) % 4, dc))
        cps.append(remote(stats.at[row], stats.at[row], ssem_s.at[i], ssem_r.at[j], line(dy, dc)))
    for cp in cps:
        cp.wait_recv()
    col_sums, squares, col_max = stats[0, 0:1, :], stats[0, 1:2, :], stats[0, 2:3, :]
    for i in range(1, 8):
        col_sums = col_sums + stats[i, 0:1, :]
        squares = squares + stats[i, 1:2, :]
        col_max = jnp.maximum(col_max, stats[i, 2:3, :])
    stat_ref[...] = jnp.broadcast_to(col_sums, (8, W))
    peak = jnp.max(col_max / col_sums - squares / (col_sums * col_sums), axis=1, keepdims=True)
    peaks[0] = jnp.broadcast_to(peak, (8, T))
    cps = []
    for i, o in enumerate(OFFS[1:]):
        j = OFFS[1:].index(((-o[0]) % 4, (-o[1]) % 4))
        cps.append(remote(peaks.at[0], peaks.at[1 + j], csem_s.at[i], csem_r.at[j], plane(*o)))
    for cp in cps:
        cp.wait_recv()
    best = peaks[0]
    for i in range(1, 16):
        best = jnp.maximum(best, peaks[i])
    chaos_ref[...] = best
    for cp in sends:
        cp.wait_send()
    out_cp.wait()


def body(transition, tile_pattern, kept_tiles):
    pos, tile_map = pl.pallas_call(
        index_kernel,
        out_shape=(jax.ShapeDtypeStruct((1, T), jnp.int32), jax.ShapeDtypeStruct((8, T), jnp.int32)),
        in_specs=[pl.BlockSpec(memory_space=pltpu.SMEM)],
        out_specs=(pl.BlockSpec(memory_space=pltpu.SMEM), pl.BlockSpec(memory_space=pltpu.SMEM)),
    )(tile_pattern)
    a = transition.reshape(RT, T, KW)
    dma = pltpu.SemaphoreType.DMA
    inflated, col_sums, chaos = pl.pallas_call(
        main_kernel,
        out_shape=(
            jax.ShapeDtypeStruct((ROWS, W), jnp.float32),
            jax.ShapeDtypeStruct((8, W), jnp.float32),
            jax.ShapeDtypeStruct((8, T), jnp.float32),
        ),
        in_specs=[
            pl.BlockSpec(memory_space=pltpu.SMEM),
            pl.BlockSpec(memory_space=pltpu.SMEM),
            pl.BlockSpec(memory_space=pl.ANY),
            pl.BlockSpec(memory_space=pl.ANY),
        ],
        out_specs=(
            pl.BlockSpec(memory_space=pl.ANY),
            pl.BlockSpec(memory_space=pltpu.VMEM),
            pl.BlockSpec(memory_space=pltpu.VMEM),
        ),
        scratch_shapes=[pltpu.VMEM((SLOTS + 1, T, T), jnp.bfloat16)] * 16
        + [
            pltpu.VMEM((RT * KT, T, T), jnp.bfloat16),
            pltpu.VMEM((8 * ROWS, W), jnp.bfloat16),
            pltpu.VMEM((ROWS, W), jnp.float32),
            pltpu.VMEM((ROWS, KW), jnp.bfloat16),
            pltpu.VMEM((16, 8, T), jnp.int32),
            pltpu.SMEM((16, 8, T), jnp.int32),
            pltpu.VMEM((8, 8, W), jnp.float32),
            pltpu.VMEM((16, 8, T), jnp.float32),
            dma((KT + 1,)),
            dma((40,)), dma((40,)),
            dma((9,)), dma((9,)),
            dma((15,)), dma((15,)),
            dma((7,)), dma((7,)),
            dma((15,)), dma((15,)),
        ],
        compiler_params=pltpu.CompilerParams(
            collective_id=0, has_side_effects=True, vmem_limit_bytes=56 * 2**20),
        cost_estimate=pl.CostEstimate(flops=14495514624, bytes_accessed=8 * 2**20, transcendentals=0),
    )(pos, kept_tiles, tile_map, a)
    node_count = transition.shape[0] * lax.axis_size("row")
    return inflated / col_sums[0] * node_count, chaos[0, 0] * node_count


def solution(mesh):
    placed = (P("row", "col"), P("row", "col"), P("row", "col"))
    return jax.shard_map(
        body, mesh=mesh, in_specs=placed, out_specs=(P("row", "col"), P()), check_vma=False
    )
```

```python
import jax
import jax.numpy as jnp
from jax import lax
from jax.experimental import pallas as pl
from jax.experimental.pallas import tpu as pltpu
from jax.sharding import PartitionSpec as P

MESH = pl.DeviceIdType.MESH
T = 128
RT, KT, PT = 12, 6, 3
SLOTS = 36
HALF = 18
QUART = 9
ROWS, KW, W = RT * T, KT * T, PT * T
OFFS = [(dx, dz) for dx in range(4) for dz in range(4)]


def main_kernel(pat_ref, kept_ref, a_ref, out_ref, chaos_ref, *scratch):
    bufs = dict(zip(OFFS, scratch[:16]))
    (tiles, ball, acc, dense, meta, meta_s, stats, peaks,
     loc_sem, asem_s, asem_r, bsem_s, bsem_r, msem_s, msem_r, ssem_s, ssem_r, csem_s, csem_r) = scratch[16:]
    row, col = lax.axis_index("row"), lax.axis_index("col")
    y, core = row // 2, row % 2
    x, z = col // 4, col % 4

    def plane(dx, dz):
        return (row, ((x + dx) % 4) * 4 + (z + dz) % 4)

    def line(dy, dc):
        return (((y + dy) % 4) * 2 + (core + dc) % 2, col)

    loads = [
        pltpu.make_async_copy(
            a_ref.at[:, :, pl.ds(c * T, T)], tiles.at[pl.ds(c * RT, RT)], loc_sem.at[c])
        for c in range(KT)
    ]
    for cp in loads:
        cp.start()
    barrier = pltpu.get_barrier_semaphore()
    others = [plane(*o) for o in OFFS[1:]] + [line(dy, dc) for dy in range(4) for dc in range(2) if (dy, dc) != (0, 0)]
    for d in others:
        pl.semaphore_signal(barrier, inc=1, device_id=d, device_id_type=MESH)

    pat = pat_ref[...]
    lane = lax.broadcasted_iota(jnp.int32, (KT, T), 1)
    run = jnp.zeros((1, RT), jnp.int32)
    below = []
    for c in range(KT):
        run = run + pat[c:c + 1, :]
        below.append(run)
    count = jnp.concatenate(below, axis=0)
    for r in range(RT - 1):
        count = count + jnp.where(lane[:, :RT] > r, run[:, r:r + 1], 0)
    ends = jnp.zeros((KT, T), jnp.int32)
    for r in range(RT):
        ends = ends + jnp.where(count[:, r:r + 1] <= lane, 1, 0)
    pos = ends[0:1, :]
    for c in range(1, KT):
        pos = pos + ends[c:c + 1, :]
    meta[0] = jnp.zeros((16, T), jnp.int32)
    meta[0, 0:KT, 0:RT] = jnp.where(pat > 0, count - 1, SLOTS)
    meta[0, KT:KT + 1, :] = jnp.minimum(pos, RT * KT - 1)
    meta[0, 8:8 + PT, 0:RT] = kept_ref[...]
    own_meta = pltpu.make_async_copy(meta.at[0], meta_s.at[0], loc_sem.at[KT])
    own_meta.start()
    for o in OFFS:
        bufs[o][SLOTS] = jnp.zeros((T, T), jnp.bfloat16)
    own_meta.wait()
    for cp in loads:
        cp.wait()
    own = bufs[(0, 0)]

    def pack(s, carry):
        p = meta_s[0, KT, s]
        own[s] = tiles[p % KT * RT + p // KT]
        return carry

    sends = []

    def remote(src, dst, s_sem, r_sem, dev):
        cp = pltpu.make_async_remote_copy(
            src_ref=src, dst_ref=dst, send_sem=s_sem, recv_sem=r_sem, device_id=dev, device_id_type=MESH)
        cp.start()
        sends.append(cp)
        return cp

    used = {}
    acount = [0]

    def apiece(src_off, axis, sign, lo, n):
        d = [0, 0]
        d[axis] = sign
        dst_off = list(src_off)
        dst_off[axis] = (dst_off[axis] - sign) % 4
        k = acount[0]
        acount[0] += 1
        cp = remote(
            bufs[src_off].at[pl.ds(lo, n)], bufs[tuple(dst_off)].at[pl.ds(lo, n)],
            asem_s.at[k], asem_r.at[k], plane(*d))
        used[(tuple(dst_off), axis, sign, lo)] = cp

    def await_piece(off, axis, sign, lo):
        used[(off, axis, sign, lo)].wait_recv()

    def off(axis, a, b):
        return (a, b) if axis == 0 else (b, a)

    lax.fori_loop(0, SLOTS, pack, 0)
    pl.semaphore_wait(barrier, len(others))

    def spread(h, axis, o):
        apiece(o, axis, 1, h * HALF, HALF)
        apiece(o, axis, -1, h * HALF, HALF)

    def got(h, axis, o1, o3):
        await_piece(o3, axis, 1, h * HALF)
        apiece(o3, axis, 1, h * HALF, QUART)
        await_piece(o1, axis, -1, h * HALF)
        apiece(o1, axis, -1, h * HALF + QUART, QUART)

    def far(h, axis, o2):
        await_piece(o2, axis, 1, h * HALF)
        await_piece(o2, axis, -1, h * HALF + QUART)

    for h in range(2):
        spread(h, h, (0, 0))
    metas = []
    for i, o in enumerate(OFFS[1:]):
        j = OFFS[1:].index(((-o[0]) % 4, (-o[1]) % 4))
        metas.append(remote(meta.at[0], meta.at[1 + j], msem_s.at[i], msem_r.at[j], plane(*o)))
    def own_panel(r, carry):
        for c in range(PT):
            ball[pl.ds(row * ROWS + r * T, T), c * T:(c + 1) * T] = own[meta_s[0, c, r]]
        return carry

    lax.fori_loop(0, RT, own_panel, 0)

    def bcopy(k, dy_src, core_src, lo, n, dev):
        blk = ball.at[pl.ds((((y + dy_src) % 4) * 2 + core_src) * ROWS + lo, n)]
        return remote(blk, blk, bsem_s.at[k], bsem_r.at[k], dev)

    HB = ROWS // 2
    b_up = bcopy(0, 0, core, 0, ROWS, line(1, 0))
    b_dn = bcopy(1, 0, core, 0, ROWS, line(-1, 0))
    b_sib = [bcopy(2, 0, core, 0, ROWS, line(0, 1))]
    for h in range(2):
        spread(h, 1 - h, (0, 0))
    for h in range(2):
        got(h, h, off(h, 1, 0), off(h, 3, 0))
    for h in range(2):
        spread(h, 1 - h, off(h, 1, 0))
        spread(h, 1 - h, off(h, 3, 0))
    b_up.wait_recv()
    b_up2 = bcopy(3, 3, core, 0, HB, line(1, 0))
    b_sib.append(bcopy(4, 3, core, 0, ROWS, line(0, 1)))
    b_dn.wait_recv()
    b_dn2 = bcopy(5, 1, core, HB, HB, line(-1, 0))
    b_sib.append(bcopy(6, 1, core, 0, ROWS, line(0, 1)))
    for h in range(2):
        far(h, h, off(h, 2, 0))
    for h in range(2):
        got(h, 1 - h, off(h, 0, 1), off(h, 0, 3))
    for h in range(2):
        spread(h, 1 - h, off(h, 2, 0))
    for cp in metas:
        cp.wait_recv()
    cp = pltpu.make_async_copy(meta.at[pl.ds(1, 15)], meta_s.at[pl.ds(1, 15)], loc_sem.at[KT])
    cp.start()
    cp.wait()
    b_up2.wait_recv()
    b_sib.append(bcopy(7, 2, core, 0, HB, line(0, 1)))
    b_dn2.wait_recv()
    b_sib.append(bcopy(8, 2, core, HB, HB, line(0, 1)))
    for cp in b_sib:
        cp.wait_recv()

    first = [True]

    def multiply(o):
        buf, m = bufs[o], OFFS.index(o)
        zero = first[0]
        first[0] = False
        src = ((x + o[0]) % 4) * 4 + (z + o[1]) % 4

        for r in range(RT):
            for c in range(KT):
                dense[r * T:(r + 1) * T, c * T:(c + 1) * T] = buf[meta_s[m, c, r]]
        p = jnp.dot(dense[...], ball[pl.ds(src * KW, KW), :], preferred_element_type=jnp.float32)
        if zero:
            acc[...] = p
        else:
            acc[...] += p

    for o in ((0, 0), (1, 0), (3, 0), (0, 1), (0, 3)):
        multiply(o)
    for s in (1, 3):
        for h in range(2):
            got(h, 1 - h, off(h, s, 1), off(h, s, 3))
    for h in range(2):
        far(h, 1 - h, off(h, 0, 2))
    for o in ((2, 0), (0, 2), (1, 1), (1, 3), (3, 1), (3, 3)):
        multiply(o)
    for h in range(2):
        got(h, 1 - h, off(h, 2, 1), off(h, 2, 3))
    for s in (1, 3):
        for h in range(2):
            far(h, 1 - h, off(h, s, 2))
    for o in ((1, 2), (3, 2), (2, 1), (2, 3)):
        multiply(o)
    for h in range(2):
        far(h, 1 - h, off(h, 2, 2))
    multiply((2, 2))

    sums = [jnp.zeros((8, T), jnp.float32)] * PT
    sqs = [jnp.zeros((8, T), jnp.float32)] * PT
    mxs = [jnp.zeros((8, T), jnp.float32)] * PT

    def finish(r, carry):
        out = []
        for c in range(PT):
            s, q, m = carry[c]
            sl = (pl.ds(r * T, T), slice(c * T, (c + 1) * T))
            v = acc[sl] * meta_s[0, 8 + c, r].astype(jnp.float32)
            v = v * v
            acc[sl] = v
            v8 = v.reshape(T // 8, 8, T)
            out.append((s + jnp.sum(v8, axis=0), q + jnp.sum(v8 * v8, axis=0), jnp.maximum(m, jnp.max(v8, axis=0))))
        return tuple(out)

    fin = lax.fori_loop(0, RT, finish, tuple((sums[c], sqs[c], mxs[c]) for c in range(PT)))
    for c in range(PT):
        s, q, m = fin[c]
        stats[row, 0:1, c * T:(c + 1) * T] = jnp.sum(s, axis=0, keepdims=True)
        stats[row, 1:2, c * T:(c + 1) * T] = jnp.sum(q, axis=0, keepdims=True)
        stats[row, 2:3, c * T:(c + 1) * T] = jnp.max(m, axis=0, keepdims=True)
    lines = [(dy, dc) for dy in range(4) for dc in range(2) if (dy, dc) != (0, 0)]
    cps = []
    for i, (dy, dc) in enumerate(lines):
        j = lines.index(((-dy) % 4, dc))
        cps.append(remote(stats.at[row], stats.at[row], ssem_s.at[i], ssem_r.at[j], line(dy, dc)))
    for cp in cps:
        cp.wait_recv()
    col_sums, squares, col_max = stats[0, 0:1, :], stats[0, 1:2, :], stats[0, 2:3, :]
    for i in range(1, 8):
        col_sums = col_sums + stats[i, 0:1, :]
        squares = squares + stats[i, 1:2, :]
        col_max = jnp.maximum(col_max, stats[i, 2:3, :])
    peak = jnp.max(col_max / col_sums - squares / (col_sums * col_sums), axis=1, keepdims=True)
    peaks[0] = jnp.broadcast_to(peak, (8, T))
    cps = []
    for i, o in enumerate(OFFS[1:]):
        j = OFFS[1:].index(((-o[0]) % 4, (-o[1]) % 4))
        cps.append(remote(peaks.at[0], peaks.at[1 + j], csem_s.at[i], csem_r.at[j], plane(*o)))
    inverse = 1.0 / col_sums
    nodes = float(8 * ROWS)
    out_cps = []
    for i in range(4):
        sl = pl.ds(i * (ROWS // 4), ROWS // 4)
        acc[sl, :] = acc[sl, :] * inverse * nodes
        out_cps.append(pltpu.make_async_copy(acc.at[sl], out_ref.at[sl], loc_sem.at[i]))
        out_cps[-1].start()
    for cp in cps:
        cp.wait_recv()
    best = peaks[0]
    for i in range(1, 16):
        best = jnp.maximum(best, peaks[i])
    chaos_ref[0, 0] = jnp.max(best) * nodes
    for cp in sends:
        cp.wait_send()
    for cp in out_cps:
        cp.wait()


def body(transition, tile_pattern, kept_tiles):
    a = transition.reshape(RT, T, KW)
    dma = pltpu.SemaphoreType.DMA
    panel, chaos = pl.pallas_call(
        main_kernel,
        out_shape=(
            jax.ShapeDtypeStruct((ROWS, W), jnp.float32),
            jax.ShapeDtypeStruct((1, 1), jnp.float32),
        ),
        in_specs=[
            pl.BlockSpec(memory_space=pltpu.VMEM),
            pl.BlockSpec(memory_space=pltpu.VMEM),
            pl.BlockSpec(memory_space=pl.ANY),
        ],
        out_specs=(
            pl.BlockSpec(memory_space=pl.ANY),
            pl.BlockSpec(memory_space=pltpu.SMEM),
        ),
        scratch_shapes=[pltpu.VMEM((SLOTS + 1, T, T), jnp.bfloat16)] * 16
        + [
            pltpu.VMEM((RT * KT, T, T), jnp.bfloat16),
            pltpu.VMEM((8 * ROWS, W), jnp.bfloat16),
            pltpu.VMEM((ROWS, W), jnp.float32),
            pltpu.VMEM((ROWS, KW), jnp.bfloat16),
            pltpu.VMEM((16, 16, T), jnp.int32),
            pltpu.SMEM((16, 16, T), jnp.int32),
            pltpu.VMEM((8, 8, W), jnp.float32),
            pltpu.VMEM((16, 8, T), jnp.float32),
            dma((KT + 1,)),
            dma((40,)), dma((40,)),
            dma((9,)), dma((9,)),
            dma((15,)), dma((15,)),
            dma((7,)), dma((7,)),
            dma((15,)), dma((15,)),
        ],
        compiler_params=pltpu.CompilerParams(
            collective_id=0, has_side_effects=True, vmem_limit_bytes=56 * 2**20),
        cost_estimate=pl.CostEstimate(flops=14495514624, bytes_accessed=8 * 2**20, transcendentals=0),
    )(tile_pattern.T, kept_tiles.T, a)
    return panel, chaos.reshape(())


def solution(mesh):
    placed = (P("row", "col"), P("row", "col"), P("row", "col"))
    return jax.shard_map(
        body, mesh=mesh, in_specs=placed, out_specs=(P("row", "col"), P()), check_vma=False
    )
```

```python
import jax
import jax.numpy as jnp
from jax import lax
from jax.experimental import pallas as pl
from jax.experimental.pallas import tpu as pltpu
from jax.sharding import PartitionSpec as P

MESH = pl.DeviceIdType.MESH
T = 128
RT, KT, PT = 12, 6, 3
SLOTS = 36
HALF = 18
QUART = 9
ROWS, KW, W = RT * T, KT * T, PT * T
OFFS = [(dx, dz) for dx in range(4) for dz in range(4)]


def main_kernel(pat_ref, kept_ref, a_ref, out_ref, chaos_ref, *scratch):
    bufs = dict(zip(OFFS, scratch[:16]))
    (tiles, ball, acc, dense, meta, meta_s, stats, peaks, pat_v, kept_v,
     loc_sem, asem_s, asem_r, bsem_s, bsem_r, msem_s, msem_r, ssem_s, ssem_r, csem_s, csem_r) = scratch[16:]
    row, col = lax.axis_index("row"), lax.axis_index("col")
    y, core = row // 2, row % 2
    x, z = col // 4, col % 4

    def plane(dx, dz):
        return (row, ((x + dx) % 4) * 4 + (z + dz) % 4)

    def line(dy, dc):
        return (((y + dy) % 4) * 2 + (core + dc) % 2, col)

    barrier = pltpu.get_barrier_semaphore()
    others = [plane(*o) for o in OFFS[1:]] + [line(dy, dc) for dy in range(4) for dc in range(2) if (dy, dc) != (0, 0)]
    for d in others:
        pl.semaphore_signal(barrier, inc=1, device_id=d, device_id_type=MESH)
    small = [
        pltpu.make_async_copy(pat_ref, pat_v, loc_sem.at[KT]),
        pltpu.make_async_copy(kept_ref, kept_v, loc_sem.at[KT + 1]),
    ]
    loads = [
        pltpu.make_async_copy(
            a_ref.at[:, :, pl.ds(c * T, T)], tiles.at[pl.ds(c * RT, RT)], loc_sem.at[c])
        for c in range(KT)
    ]
    for cp in small + loads:
        cp.start()
    for o in OFFS:
        bufs[o][SLOTS] = jnp.zeros((T, T), jnp.bfloat16)
    for cp in small:
        cp.wait()

    pat = pat_v[...]
    lane = lax.broadcasted_iota(jnp.int32, (KT, T), 1)
    run = jnp.zeros((1, RT), jnp.int32)
    below = []
    for c in range(KT):
        run = run + pat[c:c + 1, :]
        below.append(run)
    count = jnp.concatenate(below, axis=0)
    for r in range(RT - 1):
        count = count + jnp.where(lane[:, :RT] > r, run[:, r:r + 1], 0)
    ends = jnp.zeros((KT, T), jnp.int32)
    for r in range(RT):
        ends = ends + jnp.where(count[:, r:r + 1] <= lane, 1, 0)
    pos = ends[0:1, :]
    for c in range(1, KT):
        pos = pos + ends[c:c + 1, :]
    meta[0] = jnp.zeros((16, T), jnp.int32)
    meta[0, 0:KT, 0:RT] = jnp.where(pat > 0, count - 1, SLOTS)
    meta[0, KT:KT + 1, :] = jnp.minimum(pos, RT * KT - 1)
    meta[0, 8:8 + PT, 0:RT] = kept_v[...]
    own_meta = pltpu.make_async_copy(meta.at[0], meta_s.at[0], loc_sem.at[KT])
    own_meta.start()
    own_meta.wait()
    for cp in loads:
        cp.wait()
    own = bufs[(0, 0)]

    def pack(s, carry):
        p = meta_s[0, KT, s]
        own[s] = tiles[p % KT * RT + p // KT]
        return carry

    sends = []

    def remote(src, dst, s_sem, r_sem, dev):
        cp = pltpu.make_async_remote_copy(
            src_ref=src, dst_ref=dst, send_sem=s_sem, recv_sem=r_sem, device_id=dev, device_id_type=MESH)
        cp.start()
        sends.append(cp)
        return cp

    used = {}
    acount = [0]

    def apiece(src_off, axis, sign, lo, n):
        d = [0, 0]
        d[axis] = sign
        dst_off = list(src_off)
        dst_off[axis] = (dst_off[axis] - sign) % 4
        k = acount[0]
        acount[0] += 1
        cp = remote(
            bufs[src_off].at[pl.ds(lo, n)], bufs[tuple(dst_off)].at[pl.ds(lo, n)],
            asem_s.at[k], asem_r.at[k], plane(*d))
        used[(tuple(dst_off), axis, sign, lo)] = cp

    def await_piece(off, axis, sign, lo):
        used[(off, axis, sign, lo)].wait_recv()

    def off(axis, a, b):
        return (a, b) if axis == 0 else (b, a)

    lax.fori_loop(0, SLOTS, pack, 0)
    pl.semaphore_wait(barrier, len(others))

    def spread(h, axis, o):
        apiece(o, axis, 1, h * HALF, HALF)
        apiece(o, axis, -1, h * HALF, HALF)

    def got(h, axis, o1, o3):
        await_piece(o3, axis, 1, h * HALF)
        apiece(o3, axis, 1, h * HALF, QUART)
        await_piece(o1, axis, -1, h * HALF)
        apiece(o1, axis, -1, h * HALF + QUART, QUART)

    def far(h, axis, o2):
        await_piece(o2, axis, 1, h * HALF)
        await_piece(o2, axis, -1, h * HALF + QUART)

    def mcopy(k, lo, n, to, dev):
        return remote(meta.at[pl.ds(lo, n)], meta.at[pl.ds(to, n)], msem_s.at[k], msem_r.at[k], dev)

    m_x = [mcopy(0, 0, 1, 3, plane(1, 0)), mcopy(1, 0, 1, 1, plane(3, 0))]

    for h in range(2):
        spread(h, h, (0, 0))
    def own_panel(r, carry):
        for c in range(PT):
            ball[pl.ds(row * ROWS + r * T, T), c * T:(c + 1) * T] = own[meta_s[0, c, r]]
        return carry

    lax.fori_loop(0, RT, own_panel, 0)

    def bcopy(k, dy_src, core_src, lo, n, dev):
        blk = ball.at[pl.ds((((y + dy_src) % 4) * 2 + core_src) * ROWS + lo, n)]
        return remote(blk, blk, bsem_s.at[k], bsem_r.at[k], dev)

    HB = ROWS // 2
    b_up = bcopy(0, 0, core, 0, ROWS, line(1, 0))
    b_dn = bcopy(1, 0, core, 0, ROWS, line(-1, 0))
    b_sib = [bcopy(2, 0, core, 0, ROWS, line(0, 1))]
    for h in range(2):
        spread(h, 1 - h, (0, 0))
    for cp in m_x:
        cp.wait_recv()
    m_x2 = mcopy(2, 3, 1, 2, plane(1, 0))
    for h in range(2):
        got(h, h, off(h, 1, 0), off(h, 3, 0))
    m_x2.wait_recv()
    m_z = [mcopy(3, 0, 4, 12, plane(0, 1)), mcopy(4, 0, 4, 4, plane(0, 3))]
    for h in range(2):
        spread(h, 1 - h, off(h, 1, 0))
        spread(h, 1 - h, off(h, 3, 0))
    b_up.wait_recv()
    b_up2 = bcopy(3, 3, core, 0, HB, line(1, 0))
    b_sib.append(bcopy(4, 3, core, 0, ROWS, line(0, 1)))
    b_dn.wait_recv()
    b_dn2 = bcopy(5, 1, core, HB, HB, line(-1, 0))
    b_sib.append(bcopy(6, 1, core, 0, ROWS, line(0, 1)))
    for h in range(2):
        far(h, h, off(h, 2, 0))
    for h in range(2):
        got(h, 1 - h, off(h, 0, 1), off(h, 0, 3))
    for h in range(2):
        spread(h, 1 - h, off(h, 2, 0))
    for cp in m_z:
        cp.wait_recv()
    m_z2 = mcopy(5, 12, 4, 8, plane(0, 1))

    def fetch_maps(lo):
        cp = pltpu.make_async_copy(meta.at[pl.ds(lo, 4)], meta_s.at[pl.ds(lo, 4)], loc_sem.at[KT])
        cp.start()
        cp.wait()

    for lo in (0, 4, 12):
        fetch_maps(lo)
    b_up2.wait_recv()
    b_sib.append(bcopy(7, 2, core, 0, HB, line(0, 1)))
    b_dn2.wait_recv()
    b_sib.append(bcopy(8, 2, core, HB, HB, line(0, 1)))
    for cp in b_sib:
        cp.wait_recv()

    first = [True]

    def multiply(o):
        buf, m = bufs[o], o[1] * 4 + o[0]
        zero = first[0]
        first[0] = False
        src = ((x + o[0]) % 4) * 4 + (z + o[1]) % 4

        for r in range(RT):
            for c in range(KT):
                dense[r * T:(r + 1) * T, c * T:(c + 1) * T] = buf[meta_s[m, c, r]]
        p = jnp.dot(dense[...], ball[pl.ds(src * KW, KW), :], preferred_element_type=jnp.float32)
        if zero:
            acc[...] = p
        else:
            acc[...] += p

    for o in ((0, 0), (1, 0), (3, 0), (0, 1), (0, 3)):
        multiply(o)
    for s in (1, 3):
        for h in range(2):
            got(h, 1 - h, off(h, s, 1), off(h, s, 3))
    for h in range(2):
        far(h, 1 - h, off(h, 0, 2))
    m_z2.wait_recv()
    fetch_maps(8)
    for o in ((2, 0), (0, 2), (1, 1), (1, 3), (3, 1), (3, 3)):
        multiply(o)
    for h in range(2):
        got(h, 1 - h, off(h, 2, 1), off(h, 2, 3))
    for s in (1, 3):
        for h in range(2):
            far(h, 1 - h, off(h, s, 2))
    for o in ((1, 2), (3, 2), (2, 1), (2, 3)):
        multiply(o)
    for h in range(2):
        far(h, 1 - h, off(h, 2, 2))
    multiply((2, 2))

    sums = [jnp.zeros((8, T), jnp.float32)] * PT
    sqs = [jnp.zeros((8, T), jnp.float32)] * PT
    mxs = [jnp.zeros((8, T), jnp.float32)] * PT

    def finish(r, carry):
        out = []
        for c in range(PT):
            s, q, m = carry[c]
            sl = (pl.ds(r * T, T), slice(c * T, (c + 1) * T))
            v = acc[sl] * meta_s[0, 8 + c, r].astype(jnp.float32)
            v = v * v
            acc[sl] = v
            v8 = v.reshape(T // 8, 8, T)
            out.append((s + jnp.sum(v8, axis=0), q + jnp.sum(v8 * v8, axis=0), jnp.maximum(m, jnp.max(v8, axis=0))))
        return tuple(out)

    fin = lax.fori_loop(0, RT, finish, tuple((sums[c], sqs[c], mxs[c]) for c in range(PT)))
    for c in range(PT):
        s, q, m = fin[c]
        stats[row, 0:1, c * T:(c + 1) * T] = jnp.sum(s, axis=0, keepdims=True)
        stats[row, 1:2, c * T:(c + 1) * T] = jnp.sum(q, axis=0, keepdims=True)
        stats[row, 2:3, c * T:(c + 1) * T] = jnp.max(m, axis=0, keepdims=True)
    lines = [(dy, dc) for dy in range(4) for dc in range(2) if (dy, dc) != (0, 0)]
    cps = []
    for i, (dy, dc) in enumerate(lines):
        j = lines.index(((-dy) % 4, dc))
        cps.append(remote(stats.at[row], stats.at[row], ssem_s.at[i], ssem_r.at[j], line(dy, dc)))
    for cp in cps:
        cp.wait_recv()
    col_sums, squares, col_max = stats[0, 0:1, :], stats[0, 1:2, :], stats[0, 2:3, :]
    for i in range(1, 8):
        col_sums = col_sums + stats[i, 0:1, :]
        squares = squares + stats[i, 1:2, :]
        col_max = jnp.maximum(col_max, stats[i, 2:3, :])
    peak = jnp.max(col_max / col_sums - squares / (col_sums * col_sums), axis=1, keepdims=True)
    peaks[0] = jnp.broadcast_to(peak, (8, T))
    cps = []
    for i, o in enumerate(OFFS[1:]):
        j = OFFS[1:].index(((-o[0]) % 4, (-o[1]) % 4))
        cps.append(remote(peaks.at[0], peaks.at[1 + j], csem_s.at[i], csem_r.at[j], plane(*o)))
    inverse = 1.0 / col_sums
    nodes = float(8 * ROWS)
    out_ref[...] = acc[...] * inverse * nodes
    for cp in cps:
        cp.wait_recv()
    best = peaks[0]
    for i in range(1, 16):
        best = jnp.maximum(best, peaks[i])
    chaos_ref[0, 0] = jnp.max(best) * nodes
    for cp in sends:
        cp.wait_send()


def body(transition, tile_pattern, kept_tiles):
    a = transition.reshape(RT, T, KW)
    dma = pltpu.SemaphoreType.DMA
    panel, chaos = pl.pallas_call(
        main_kernel,
        out_shape=(
            jax.ShapeDtypeStruct((ROWS, W), jnp.float32),
            jax.ShapeDtypeStruct((1, 1), jnp.float32),
        ),
        in_specs=[
            pl.BlockSpec(memory_space=pltpu.HBM),
            pl.BlockSpec(memory_space=pltpu.HBM),
            pl.BlockSpec(memory_space=pltpu.HBM),
        ],
        out_specs=(
            pl.BlockSpec(memory_space=pltpu.VMEM),
            pl.BlockSpec(memory_space=pltpu.SMEM),
        ),
        scratch_shapes=[pltpu.VMEM((SLOTS + 1, T, T), jnp.bfloat16)] * 16
        + [
            pltpu.VMEM((RT * KT, T, T), jnp.bfloat16),
            pltpu.VMEM((8 * ROWS, W), jnp.bfloat16),
            pltpu.VMEM((ROWS, W), jnp.float32),
            pltpu.VMEM((ROWS, KW), jnp.bfloat16),
            pltpu.VMEM((16, 16, T), jnp.int32),
            pltpu.SMEM((16, 16, T), jnp.int32),
            pltpu.VMEM((8, 8, W), jnp.float32),
            pltpu.VMEM((16, 8, T), jnp.float32),
            pltpu.VMEM((KT, RT), jnp.int32),
            pltpu.VMEM((PT, RT), jnp.int32),
            dma((KT + 2,)),
            dma((40,)), dma((40,)),
            dma((9,)), dma((9,)),
            dma((6,)), dma((6,)),
            dma((7,)), dma((7,)),
            dma((15,)), dma((15,)),
        ],
        compiler_params=pltpu.CompilerParams(
            collective_id=0, has_side_effects=True, vmem_limit_bytes=50 * 2**20),
        cost_estimate=pl.CostEstimate(flops=14495514624, bytes_accessed=8 * 2**20, transcendentals=0),
    )(tile_pattern.T, kept_tiles.T, a)
    return panel, chaos.reshape(())


def solution(mesh):
    placed = (P("row", "col"), P("row", "col"), P("row", "col"))
    return jax.shard_map(
        body, mesh=mesh, in_specs=placed, out_specs=(P("row", "col"), P()), check_vma=False
    )
```

```python
import jax
import jax.numpy as jnp
from jax import lax
from jax.experimental import pallas as pl
from jax.experimental.pallas import tpu as pltpu
from jax.sharding import PartitionSpec as P

MESH = pl.DeviceIdType.MESH
T = 128
RT, KT, PT = 12, 6, 3
SLOTS = 36
HALF = 18
QUART = 9
ROWS, KW, W = RT * T, KT * T, PT * T
OFFS = [(dx, dz) for dx in range(4) for dz in range(4)]


def main_kernel(pat_ref, kept_ref, a_ref, out_ref, chaos_ref, *scratch):
    bufs = dict(zip(OFFS, scratch[:16]))
    (tiles, ball, acc, dense, meta, meta_s, stats, peaks,
     loc_sem, asem_s, asem_r, bsem_s, bsem_r, msem_s, msem_r, ssem_s, ssem_r, csem_s, csem_r) = scratch[16:]
    row, col = lax.axis_index("row"), lax.axis_index("col")
    y, core = row // 2, row % 2
    x, z = col // 4, col % 4

    def plane(dx, dz):
        return (row, ((x + dx) % 4) * 4 + (z + dz) % 4)

    def line(dy, dc):
        return (((y + dy) % 4) * 2 + (core + dc) % 2, col)

    barrier = pltpu.get_barrier_semaphore()
    others = [plane(*o) for o in OFFS[1:]] + [line(dy, dc) for dy in range(4) for dc in range(2) if (dy, dc) != (0, 0)]
    for d in others:
        pl.semaphore_signal(barrier, inc=1, device_id=d, device_id_type=MESH)
    loads = [
        pltpu.make_async_copy(
            a_ref.at[:, :, pl.ds(c * T, T)], tiles.at[pl.ds(c * RT, RT)], loc_sem.at[c])
        for c in range(KT)
    ]
    for cp in loads:
        cp.start()
    lane = lax.broadcasted_iota(jnp.int32, (1, T), 1)
    count = jnp.int32(0)
    pos = jnp.zeros((1, T), jnp.int32)
    maps = [pos] * KT
    for r in range(RT):
        for c in range(KT):
            v = pat_ref[c, r]
            maps[c] = jnp.where(lane == r, jnp.where(v > 0, count, SLOTS), maps[c])
            count = count + v
            pos = pos + jnp.where(count <= lane, 1, 0)
    for c in range(KT):
        meta[0, c:c + 1, :] = maps[c]
    meta[0, KT:KT + 1, :] = jnp.minimum(pos, RT * KT - 1)
    meta[0, KT + 1:8, :] = jnp.zeros((1, T), jnp.int32)
    own_meta = pltpu.make_async_copy(meta.at[0], meta_s.at[0], loc_sem.at[KT])
    own_meta.start()
    for o in OFFS:
        bufs[o][SLOTS] = jnp.zeros((T, T), jnp.bfloat16)
    own_meta.wait()
    for cp in loads:
        cp.wait()
    own = bufs[(0, 0)]

    def pack(s, carry):
        p = meta_s[0, KT, s]
        own[s] = tiles[p % KT * RT + p // KT]
        return carry

    sends = []

    def remote(src, dst, s_sem, r_sem, dev):
        cp = pltpu.make_async_remote_copy(
            src_ref=src, dst_ref=dst, send_sem=s_sem, recv_sem=r_sem, device_id=dev, device_id_type=MESH)
        cp.start()
        sends.append(cp)
        return cp

    used = {}
    acount = [0]

    def apiece(src_off, axis, sign, lo, n):
        d = [0, 0]
        d[axis] = sign
        dst_off = list(src_off)
        dst_off[axis] = (dst_off[axis] - sign) % 4
        k = acount[0]
        acount[0] += 1
        cp = remote(
            bufs[src_off].at[pl.ds(lo, n)], bufs[tuple(dst_off)].at[pl.ds(lo, n)],
            asem_s.at[k], asem_r.at[k], plane(*d))
        used[(tuple(dst_off), axis, sign, lo)] = cp

    def await_piece(off, axis, sign, lo):
        used[(off, axis, sign, lo)].wait_recv()

    def off(axis, a, b):
        return (a, b) if axis == 0 else (b, a)

    lax.fori_loop(0, HALF, pack, 0)
    pl.semaphore_wait(barrier, len(others))

    def spread(h, axis, o):
        apiece(o, axis, 1, h * HALF, HALF)
        apiece(o, axis, -1, h * HALF, HALF)

    def got(h, axis, o1, o3):
        await_piece(o3, axis, 1, h * HALF)
        apiece(o3, axis, 1, h * HALF, QUART)
        await_piece(o1, axis, -1, h * HALF)
        apiece(o1, axis, -1, h * HALF + QUART, QUART)

    def far(h, axis, o2):
        await_piece(o2, axis, 1, h * HALF)
        await_piece(o2, axis, -1, h * HALF + QUART)

    def mcopy(k, lo, n, to, dev):
        return remote(meta.at[pl.ds(lo, n)], meta.at[pl.ds(to, n)], msem_s.at[k], msem_r.at[k], dev)

    m_x = [mcopy(0, 0, 1, 3, plane(1, 0)), mcopy(1, 0, 1, 1, plane(3, 0))]

    spread(0, 0, (0, 0))
    lax.fori_loop(HALF, SLOTS, pack, 0)
    spread(1, 1, (0, 0))
    def own_panel(r, carry):
        for c in range(PT):
            ball[pl.ds(row * ROWS + r * T, T), c * T:(c + 1) * T] = own[meta_s[0, c, r]]
        return carry

    lax.fori_loop(0, RT, own_panel, 0)

    def bcopy(k, dy_src, core_src, lo, n, dev):
        blk = ball.at[pl.ds((((y + dy_src) % 4) * 2 + core_src) * ROWS + lo, n)]
        return remote(blk, blk, bsem_s.at[k], bsem_r.at[k], dev)

    HB = ROWS // 2
    b_up = bcopy(0, 0, core, 0, ROWS, line(1, 0))
    b_dn = bcopy(1, 0, core, 0, ROWS, line(-1, 0))
    b_sib = [bcopy(2, 0, core, 0, ROWS, line(0, 1))]
    for h in range(2):
        spread(h, 1 - h, (0, 0))
    for cp in m_x:
        cp.wait_recv()
    m_x2 = mcopy(2, 3, 1, 2, plane(1, 0))
    for h in range(2):
        got(h, h, off(h, 1, 0), off(h, 3, 0))
    m_x2.wait_recv()
    m_z = [mcopy(3, 0, 4, 12, plane(0, 1)), mcopy(4, 0, 4, 4, plane(0, 3))]
    for h in range(2):
        spread(h, 1 - h, off(h, 1, 0))
        spread(h, 1 - h, off(h, 3, 0))
    b_up.wait_recv()
    b_up2 = bcopy(3, 3, core, 0, HB, line(1, 0))
    b_sib.append(bcopy(4, 3, core, 0, ROWS, line(0, 1)))
    b_dn.wait_recv()
    b_dn2 = bcopy(5, 1, core, HB, HB, line(-1, 0))
    b_sib.append(bcopy(6, 1, core, 0, ROWS, line(0, 1)))
    for h in range(2):
        far(h, h, off(h, 2, 0))
    for h in range(2):
        got(h, 1 - h, off(h, 0, 1), off(h, 0, 3))
    for h in range(2):
        spread(h, 1 - h, off(h, 2, 0))
    for cp in m_z:
        cp.wait_recv()
    m_z2 = mcopy(5, 12, 4, 8, plane(0, 1))

    def fetch_maps(lo):
        cp = pltpu.make_async_copy(meta.at[pl.ds(lo, 4)], meta_s.at[pl.ds(lo, 4)], loc_sem.at[KT])
        cp.start()
        cp.wait()

    for lo in (0, 4, 12):
        fetch_maps(lo)
    b_up2.wait_recv()
    b_sib.append(bcopy(7, 2, core, 0, HB, line(0, 1)))
    b_dn2.wait_recv()
    b_sib.append(bcopy(8, 2, core, HB, HB, line(0, 1)))
    for cp in b_sib:
        cp.wait_recv()

    first = [True]

    def multiply(o):
        buf, m = bufs[o], o[1] * 4 + o[0]
        zero = first[0]
        first[0] = False
        src = ((x + o[0]) % 4) * 4 + (z + o[1]) % 4

        for r in range(RT):
            for c in range(KT):
                dense[r * T:(r + 1) * T, c * T:(c + 1) * T] = buf[meta_s[m, c, r]]
        p = jnp.dot(dense[...], ball[pl.ds(src * KW, KW), :], preferred_element_type=jnp.float32)
        if zero:
            acc[...] = p
        else:
            acc[...] += p

    for o in ((0, 0), (1, 0), (3, 0), (0, 1), (0, 3)):
        multiply(o)
    for s in (1, 3):
        for h in range(2):
            got(h, 1 - h, off(h, s, 1), off(h, s, 3))
    for h in range(2):
        far(h, 1 - h, off(h, 0, 2))
    m_z2.wait_recv()
    fetch_maps(8)
    for o in ((2, 0), (0, 2), (1, 1), (1, 3), (3, 1), (3, 3)):
        multiply(o)
    for h in range(2):
        got(h, 1 - h, off(h, 2, 1), off(h, 2, 3))
    for s in (1, 3):
        for h in range(2):
            far(h, 1 - h, off(h, s, 2))
    for o in ((1, 2), (3, 2), (2, 1), (2, 3)):
        multiply(o)
    for h in range(2):
        far(h, 1 - h, off(h, 2, 2))
    multiply((2, 2))

    sums = [jnp.zeros((8, T), jnp.float32)] * PT
    sqs = [jnp.zeros((8, T), jnp.float32)] * PT
    mxs = [jnp.zeros((8, T), jnp.float32)] * PT

    def finish(r, carry):
        out = []
        for c in range(PT):
            s, q, m = carry[c]
            sl = (pl.ds(r * T, T), slice(c * T, (c + 1) * T))
            v = acc[sl] * kept_ref[c, r].astype(jnp.float32)
            v = v * v
            acc[sl] = v
            v8 = v.reshape(T // 8, 8, T)
            out.append((s + jnp.sum(v8, axis=0), q + jnp.sum(v8 * v8, axis=0), jnp.maximum(m, jnp.max(v8, axis=0))))
        return tuple(out)

    fin = lax.fori_loop(0, RT, finish, tuple((sums[c], sqs[c], mxs[c]) for c in range(PT)))
    for c in range(PT):
        s, q, m = fin[c]
        stats[row, 0:1, c * T:(c + 1) * T] = jnp.sum(s, axis=0, keepdims=True)
        stats[row, 1:2, c * T:(c + 1) * T] = jnp.sum(q, axis=0, keepdims=True)
        stats[row, 2:3, c * T:(c + 1) * T] = jnp.max(m, axis=0, keepdims=True)
    lines = [(dy, dc) for dy in range(4) for dc in range(2) if (dy, dc) != (0, 0)]
    cps = []
    for i, (dy, dc) in enumerate(lines):
        j = lines.index(((-dy) % 4, dc))
        cps.append(remote(stats.at[row], stats.at[row], ssem_s.at[i], ssem_r.at[j], line(dy, dc)))
    for cp in cps:
        cp.wait_recv()
    col_sums, squares, col_max = stats[0, 0:1, :], stats[0, 1:2, :], stats[0, 2:3, :]
    for i in range(1, 8):
        col_sums = col_sums + stats[i, 0:1, :]
        squares = squares + stats[i, 1:2, :]
        col_max = jnp.maximum(col_max, stats[i, 2:3, :])
    peak = jnp.max(col_max / col_sums - squares / (col_sums * col_sums), axis=1, keepdims=True)
    peaks[0] = jnp.broadcast_to(peak, (8, T))
    cps = []
    for i, o in enumerate(OFFS[1:]):
        j = OFFS[1:].index(((-o[0]) % 4, (-o[1]) % 4))
        cps.append(remote(peaks.at[0], peaks.at[1 + j], csem_s.at[i], csem_r.at[j], plane(*o)))
    inverse = 1.0 / col_sums
    nodes = float(8 * ROWS)
    out_ref[...] = acc[...] * inverse * nodes
    for cp in cps:
        cp.wait_recv()
    best = peaks[0]
    for i in range(1, 16):
        best = jnp.maximum(best, peaks[i])
    chaos_ref[0, 0] = jnp.max(best) * nodes
    for cp in sends:
        cp.wait_send()


def body(transition, tile_pattern, kept_tiles):
    a = transition.reshape(RT, T, KW)
    dma = pltpu.SemaphoreType.DMA
    panel, chaos = pl.pallas_call(
        main_kernel,
        out_shape=(
            jax.ShapeDtypeStruct((ROWS, W), jnp.float32),
            jax.ShapeDtypeStruct((1, 1), jnp.float32),
        ),
        in_specs=[
            pl.BlockSpec(memory_space=pltpu.SMEM),
            pl.BlockSpec(memory_space=pltpu.SMEM),
            pl.BlockSpec(memory_space=pltpu.HBM),
        ],
        out_specs=(
            pl.BlockSpec(memory_space=pltpu.VMEM),
            pl.BlockSpec(memory_space=pltpu.SMEM),
        ),
        scratch_shapes=[pltpu.VMEM((SLOTS + 1, T, T), jnp.bfloat16)] * 16
        + [
            pltpu.VMEM((RT * KT, T, T), jnp.bfloat16),
            pltpu.VMEM((8 * ROWS, W), jnp.bfloat16),
            pltpu.VMEM((ROWS, W), jnp.float32),
            pltpu.VMEM((ROWS, KW), jnp.bfloat16),
            pltpu.VMEM((16, 8, T), jnp.int32),
            pltpu.SMEM((16, 8, T), jnp.int32),
            pltpu.VMEM((8, 8, W), jnp.float32),
            pltpu.VMEM((16, 8, T), jnp.float32),
            dma((KT + 1,)),
            dma((40,)), dma((40,)),
            dma((9,)), dma((9,)),
            dma((6,)), dma((6,)),
            dma((7,)), dma((7,)),
            dma((15,)), dma((15,)),
        ],
        compiler_params=pltpu.CompilerParams(
            collective_id=0, has_side_effects=True, vmem_limit_bytes=50 * 2**20),
        cost_estimate=pl.CostEstimate(flops=14495514624, bytes_accessed=8 * 2**20, transcendentals=0),
    )(*(pltpu.with_memory_space_constraint(v, pltpu.HBM) for v in (tile_pattern.T, kept_tiles.T, a)))
    return panel, chaos.reshape(())


def solution(mesh):
    placed = (P("row", "col"), P("row", "col"), P("row", "col"))
    return jax.shard_map(
        body, mesh=mesh, in_specs=placed, out_specs=(P("row", "col"), P()), check_vma=False
    )
```

```python
import jax
import jax.numpy as jnp
from jax import lax
from jax.experimental import pallas as pl
from jax.experimental.pallas import tpu as pltpu
from jax.sharding import PartitionSpec as P

MESH = pl.DeviceIdType.MESH
T = 128
RT, KT, PT = 12, 6, 3
SLOTS = 36
HALF = 18
QUART = 9
ROWS, KW, W = RT * T, KT * T, PT * T
OFFS = [(dx, dz) for dx in range(4) for dz in range(4)]


def main_kernel(pat_ref, kept_ref, a_ref, out_ref, chaos_ref, *scratch):
    bufs = dict(zip(OFFS, scratch[:16]))
    (tiles, ball, acc, dense, meta, meta_s, stats, peaks,
     loc_sem, asem_s, asem_r, bsem_s, bsem_r, msem_s, msem_r, ssem_s, ssem_r, csem_s, csem_r) = scratch[16:]
    row, col = lax.axis_index("row"), lax.axis_index("col")
    y, core = row // 2, row % 2
    x, z = col // 4, col % 4

    def plane(dx, dz):
        return (row, ((x + dx) % 4) * 4 + (z + dz) % 4)

    def line(dy, dc):
        return (((y + dy) % 4) * 2 + (core + dc) % 2, col)

    barrier = pltpu.get_barrier_semaphore()
    others = [plane(*o) for o in sorted(OFFS[1:], key=lambda o: min(o[0], 4 - o[0]) + min(o[1], 4 - o[1]))]
    others += [line(dy, dc) for dy in range(4) for dc in range(2) if (dy, dc) != (0, 0)]
    for d in others:
        pl.semaphore_signal(barrier, inc=1, device_id=d, device_id_type=MESH)
    loads = [
        pltpu.make_async_copy(
            a_ref.at[:, :, pl.ds(c * T, T)], tiles.at[pl.ds(c * RT, RT)], loc_sem.at[c])
        for c in range(KT)
    ]
    for cp in loads:
        cp.start()
    lane = lax.broadcasted_iota(jnp.int32, (1, T), 1)
    count = jnp.int32(0)
    pos = jnp.zeros((1, T), jnp.int32)
    maps = [pos] * KT
    for r in range(RT):
        for c in range(KT):
            v = pat_ref[c, r]
            maps[c] = jnp.where(lane == r, jnp.where(v > 0, count, SLOTS), maps[c])
            count = count + v
            pos = pos + jnp.where(count <= lane, 1, 0)
    for c in range(KT):
        meta[0, c:c + 1, :] = maps[c]
    meta[0, KT:KT + 1, :] = jnp.minimum(pos, RT * KT - 1)
    meta[0, KT + 1:8, :] = jnp.zeros((1, T), jnp.int32)
    own_meta = pltpu.make_async_copy(meta.at[0], meta_s.at[0], loc_sem.at[KT])
    own_meta.start()
    for o in OFFS:
        bufs[o][SLOTS] = jnp.zeros((T, T), jnp.bfloat16)
    own_meta.wait()
    for cp in loads:
        cp.wait()
    own = bufs[(0, 0)]

    def pack(s, carry):
        p = meta_s[0, KT, s]
        own[s] = tiles[p % KT * RT + p // KT]
        return carry

    sends = []

    def remote(src, dst, s_sem, r_sem, dev):
        cp = pltpu.make_async_remote_copy(
            src_ref=src, dst_ref=dst, send_sem=s_sem, recv_sem=r_sem, device_id=dev, device_id_type=MESH)
        cp.start()
        sends.append(cp)
        return cp

    used = {}
    acount = [0]

    def apiece(src_off, axis, sign, lo, n):
        d = [0, 0]
        d[axis] = sign
        dst_off = list(src_off)
        dst_off[axis] = (dst_off[axis] - sign) % 4
        k = acount[0]
        acount[0] += 1
        cp = remote(
            bufs[src_off].at[pl.ds(lo, n)], bufs[tuple(dst_off)].at[pl.ds(lo, n)],
            asem_s.at[k], asem_r.at[k], plane(*d))
        used[(tuple(dst_off), axis, sign, lo)] = cp

    def await_piece(off, axis, sign, lo):
        used[(off, axis, sign, lo)].wait_recv()

    def off(axis, a, b):
        return (a, b) if axis == 0 else (b, a)

    lax.fori_loop(0, HALF, pack, 0)
    pl.semaphore_wait(barrier, len(others))

    def spread(h, axis, o):
        apiece(o, axis, 1, h * HALF, HALF)
        apiece(o, axis, -1, h * HALF, HALF)

    def got(h, axis, o1, o3):
        await_piece(o3, axis, 1, h * HALF)
        apiece(o3, axis, 1, h * HALF, QUART)
        await_piece(o1, axis, -1, h * HALF)
        apiece(o1, axis, -1, h * HALF + QUART, QUART)

    def far(h, axis, o2):
        await_piece(o2, axis, 1, h * HALF)
        await_piece(o2, axis, -1, h * HALF + QUART)

    def mcopy(k, lo, n, to, dev):
        return remote(meta.at[pl.ds(lo, n)], meta.at[pl.ds(to, n)], msem_s.at[k], msem_r.at[k], dev)

    m_x = [mcopy(0, 0, 1, 3, plane(1, 0)), mcopy(1, 0, 1, 1, plane(3, 0))]

    spread(0, 0, (0, 0))
    lax.fori_loop(HALF, SLOTS, pack, 0)
    spread(1, 1, (0, 0))
    def own_panel(r, carry):
        for c in range(PT):
            ball[pl.ds(row * ROWS + r * T, T), c * T:(c + 1) * T] = own[meta_s[0, c, r]]
        return carry

    lax.fori_loop(0, RT, own_panel, 0)

    def bcopy(k, dy_src, core_src, lo, n, dev):
        blk = ball.at[pl.ds((((y + dy_src) % 4) * 2 + core_src) * ROWS + lo, n)]
        return remote(blk, blk, bsem_s.at[k], bsem_r.at[k], dev)

    HB = ROWS // 2
    b_up = bcopy(0, 0, core, 0, ROWS, line(1, 0))
    b_dn = bcopy(1, 0, core, 0, ROWS, line(-1, 0))
    b_sib = [bcopy(2, 0, core, 0, ROWS, line(0, 1))]
    for h in range(2):
        spread(h, 1 - h, (0, 0))
    for cp in m_x:
        cp.wait_recv()
    m_x2 = mcopy(2, 3, 1, 2, plane(1, 0))
    for h in range(2):
        got(h, h, off(h, 1, 0), off(h, 3, 0))
    m_x2.wait_recv()
    m_z = [mcopy(3, 0, 4, 12, plane(0, 1)), mcopy(4, 0, 4, 4, plane(0, 3))]
    for h in range(2):
        spread(h, 1 - h, off(h, 1, 0))
        spread(h, 1 - h, off(h, 3, 0))
    b_up.wait_recv()
    b_up2 = bcopy(3, 3, core, 0, HB, line(1, 0))
    b_sib.append(bcopy(4, 3, core, 0, ROWS, line(0, 1)))
    b_dn.wait_recv()
    b_dn2 = bcopy(5, 1, core, HB, HB, line(-1, 0))
    b_sib.append(bcopy(6, 1, core, 0, ROWS, line(0, 1)))
    for h in range(2):
        far(h, h, off(h, 2, 0))
    for h in range(2):
        got(h, 1 - h, off(h, 0, 1), off(h, 0, 3))
    for h in range(2):
        spread(h, 1 - h, off(h, 2, 0))
    for cp in m_z:
        cp.wait_recv()
    m_z2 = mcopy(5, 12, 4, 8, plane(0, 1))

    def fetch_maps(lo):
        cp = pltpu.make_async_copy(meta.at[pl.ds(lo, 4)], meta_s.at[pl.ds(lo, 4)], loc_sem.at[KT])
        cp.start()
        cp.wait()

    for lo in (0, 4, 12):
        fetch_maps(lo)
    b_up2.wait_recv()
    b_sib.append(bcopy(7, 2, core, 0, HB, line(0, 1)))
    b_dn2.wait_recv()
    b_sib.append(bcopy(8, 2, core, HB, HB, line(0, 1)))
    for cp in b_sib:
        cp.wait_recv()

    first = [True]

    def multiply(o):
        buf, m = bufs[o], o[1] * 4 + o[0]
        zero = first[0]
        first[0] = False
        src = ((x + o[0]) % 4) * 4 + (z + o[1]) % 4

        for r in range(RT):
            for c in range(KT):
                dense[r * T:(r + 1) * T, c * T:(c + 1) * T] = buf[meta_s[m, c, r]]
        p = jnp.dot(dense[...], ball[pl.ds(src * KW, KW), :], preferred_element_type=jnp.float32)
        if zero:
            acc[...] = p
        else:
            acc[...] += p

    for o in ((0, 0), (1, 0), (3, 0), (0, 1), (0, 3)):
        multiply(o)
    for s in (1, 3):
        for h in range(2):
            got(h, 1 - h, off(h, s, 1), off(h, s, 3))
    for h in range(2):
        far(h, 1 - h, off(h, 0, 2))
    m_z2.wait_recv()
    fetch_maps(8)
    for o in ((2, 0), (0, 2), (1, 1)):
        multiply(o)
    for h in range(2):
        got(h, 1 - h, off(h, 2, 1), off(h, 2, 3))
    for o in ((1, 3), (3, 1), (3, 3)):
        multiply(o)
    for s in (1, 3):
        for h in range(2):
            far(h, 1 - h, off(h, s, 2))
        multiply((s, 2))
        multiply((2, s))
    for h in range(2):
        far(h, 1 - h, off(h, 2, 2))
    multiply((2, 2))

    sums = [jnp.zeros((8, T), jnp.float32)] * PT
    sqs = [jnp.zeros((8, T), jnp.float32)] * PT
    mxs = [jnp.zeros((8, T), jnp.float32)] * PT

    def finish(r, carry):
        out = []
        for c in range(PT):
            s, q, m = carry[c]
            sl = (pl.ds(r * T, T), slice(c * T, (c + 1) * T))
            v = acc[sl] * kept_ref[c, r].astype(jnp.float32)
            v = v * v
            acc[sl] = v
            v8 = v.reshape(T // 8, 8, T)
            out.append((s + jnp.sum(v8, axis=0), q + jnp.sum(v8 * v8, axis=0), jnp.maximum(m, jnp.max(v8, axis=0))))
        return tuple(out)

    fin = lax.fori_loop(0, RT, finish, tuple((sums[c], sqs[c], mxs[c]) for c in range(PT)))
    for c in range(PT):
        s, q, m = fin[c]
        stats[row, 0:1, c * T:(c + 1) * T] = jnp.sum(s, axis=0, keepdims=True)
        stats[row, 1:2, c * T:(c + 1) * T] = jnp.sum(q, axis=0, keepdims=True)
        stats[row, 2:3, c * T:(c + 1) * T] = jnp.max(m, axis=0, keepdims=True)
    lines = [(dy, dc) for dy in range(4) for dc in range(2) if (dy, dc) != (0, 0)]
    cps = []
    for i, (dy, dc) in enumerate(lines):
        j = lines.index(((-dy) % 4, dc))
        cps.append(remote(stats.at[row], stats.at[row], ssem_s.at[i], ssem_r.at[j], line(dy, dc)))
    for cp in cps:
        cp.wait_recv()
    col_sums, squares, col_max = stats[0, 0:1, :], stats[0, 1:2, :], stats[0, 2:3, :]
    for i in range(1, 8):
        col_sums = col_sums + stats[i, 0:1, :]
        squares = squares + stats[i, 1:2, :]
        col_max = jnp.maximum(col_max, stats[i, 2:3, :])
    peak = col_max / col_sums - squares / (col_sums * col_sums)
    peak = jnp.maximum(jnp.maximum(peak[:, :T], peak[:, T:2 * T]), peak[:, 2 * T:])
    peaks[0] = jnp.broadcast_to(peak, (8, T))
    cps = []
    for i, o in enumerate(OFFS[1:]):
        j = OFFS[1:].index(((-o[0]) % 4, (-o[1]) % 4))
        cps.append(remote(peaks.at[0], peaks.at[1 + j], csem_s.at[i], csem_r.at[j], plane(*o)))
    inverse = 1.0 / col_sums
    nodes = float(8 * ROWS)
    out_ref[...] = acc[...] * inverse * nodes
    for cp in sends:
        cp.wait_send()
    for cp in cps:
        cp.wait_recv()
    best = peaks[0]
    for i in range(1, 16):
        best = jnp.maximum(best, peaks[i])
    chaos_ref[0, 0] = jnp.max(best) * nodes


def body(transition, tile_pattern, kept_tiles):
    a = transition.reshape(RT, T, KW)
    dma = pltpu.SemaphoreType.DMA
    panel, chaos = pl.pallas_call(
        main_kernel,
        out_shape=(
            jax.ShapeDtypeStruct((ROWS, W), jnp.float32),
            jax.ShapeDtypeStruct((1, 1), jnp.float32),
        ),
        in_specs=[
            pl.BlockSpec(memory_space=pltpu.SMEM),
            pl.BlockSpec(memory_space=pltpu.SMEM),
            pl.BlockSpec(memory_space=pltpu.HBM),
        ],
        out_specs=(
            pl.BlockSpec(memory_space=pltpu.VMEM),
            pl.BlockSpec(memory_space=pltpu.SMEM),
        ),
        scratch_shapes=[pltpu.VMEM((SLOTS + 1, T, T), jnp.bfloat16)] * 16
        + [
            pltpu.VMEM((RT * KT, T, T), jnp.bfloat16),
            pltpu.VMEM((8 * ROWS, W), jnp.bfloat16),
            pltpu.VMEM((ROWS, W), jnp.float32),
            pltpu.VMEM((ROWS, KW), jnp.bfloat16),
            pltpu.VMEM((16, 8, T), jnp.int32),
            pltpu.SMEM((16, 8, T), jnp.int32),
            pltpu.VMEM((8, 8, W), jnp.float32),
            pltpu.VMEM((16, 8, T), jnp.float32),
            dma((KT + 1,)),
            dma((40,)), dma((40,)),
            dma((9,)), dma((9,)),
            dma((6,)), dma((6,)),
            dma((7,)), dma((7,)),
            dma((15,)), dma((15,)),
        ],
        compiler_params=pltpu.CompilerParams(
            collective_id=0, has_side_effects=True, vmem_limit_bytes=50 * 2**20),
        cost_estimate=pl.CostEstimate(flops=14495514624, bytes_accessed=8 * 2**20, transcendentals=0),
    )(*(pltpu.with_memory_space_constraint(v, pltpu.HBM) for v in (tile_pattern.T, kept_tiles.T, a)))
    return panel, chaos.reshape(())


def solution(mesh):
    placed = (P("row", "col"), P("row", "col"), P("row", "col"))
    return jax.shard_map(
        body, mesh=mesh, in_specs=placed, out_specs=(P("row", "col"), P()), check_vma=False
    )
```

```python
import jax
import jax.numpy as jnp
from jax import lax
from jax.experimental import pallas as pl
from jax.experimental.pallas import tpu as pltpu
from jax.sharding import PartitionSpec as P

MESH = pl.DeviceIdType.MESH
T = 128
RT, KT, PT = 12, 6, 3
SLOTS = 36
HALF = 18
QUART = 9
ROWS, KW, W = RT * T, KT * T, PT * T
OFFS = [(dx, dz) for dx in range(4) for dz in range(4)]


def main_kernel(pat_ref, kept_ref, a_ref, out_ref, chaos_ref, *scratch):
    bufs = dict(zip(OFFS, scratch[:16]))
    (tiles, ball, acc, dense, meta, meta_s, stats, peaks,
     loc_sem, asem_s, asem_r, bsem_s, bsem_r, msem_s, msem_r, ssem_s, ssem_r, csem_s, csem_r) = scratch[16:]
    row, col = lax.axis_index("row"), lax.axis_index("col")
    y, core = row // 2, row % 2
    x, z = col // 4, col % 4

    def plane(dx, dz):
        return (row, ((x + dx) % 4) * 4 + (z + dz) % 4)

    def line(dy, dc):
        return (((y + dy) % 4) * 2 + (core + dc) % 2, col)

    barrier = pltpu.get_barrier_semaphore()
    others = [plane(1, 0), plane(3, 0), plane(0, 1), plane(0, 3), line(1, 0), line(3, 0), line(0, 1)]
    for d in others:
        pl.semaphore_signal(barrier, inc=1, device_id=d, device_id_type=MESH)
    loads = [
        pltpu.make_async_copy(
            a_ref.at[:, :, pl.ds(c * T, T)], tiles.at[pl.ds(c * RT, RT)], loc_sem.at[c])
        for c in range(KT)
    ]
    for cp in loads:
        cp.start()
    lane = lax.broadcasted_iota(jnp.int32, (1, T), 1)
    count = jnp.int32(0)
    pos = jnp.zeros((1, T), jnp.int32)
    maps = [pos] * KT
    for r in range(RT):
        for c in range(KT):
            v = pat_ref[c, r]
            maps[c] = jnp.where(lane == r, jnp.where(v > 0, count, SLOTS), maps[c])
            count = count + v
            pos = pos + jnp.where(count <= lane, 1, 0)
    for c in range(KT):
        meta[0, c:c + 1, :] = maps[c]
    meta[0, KT:KT + 1, :] = jnp.minimum(pos, RT * KT - 1)
    meta[0, KT + 1:8, :] = jnp.zeros((1, T), jnp.int32)
    own_meta = pltpu.make_async_copy(meta.at[0], meta_s.at[0], loc_sem.at[KT])
    own_meta.start()
    for o in OFFS:
        bufs[o][SLOTS] = jnp.zeros((T, T), jnp.bfloat16)
    own_meta.wait()
    for cp in loads:
        cp.wait()
    own = bufs[(0, 0)]

    def pack(s, carry):
        p = meta_s[0, KT, s]
        own[s] = tiles[p % KT * RT + p // KT]
        return carry

    sends = []

    def remote(src, dst, s_sem, r_sem, dev):
        cp = pltpu.make_async_remote_copy(
            src_ref=src, dst_ref=dst, send_sem=s_sem, recv_sem=r_sem, device_id=dev, device_id_type=MESH)
        cp.start()
        sends.append(cp)
        return cp

    used = {}
    acount = [0]

    def apiece(src_off, axis, sign, lo, n):
        d = [0, 0]
        d[axis] = sign
        dst_off = list(src_off)
        dst_off[axis] = (dst_off[axis] - sign) % 4
        k = acount[0]
        acount[0] += 1
        cp = remote(
            bufs[src_off].at[pl.ds(lo, n)], bufs[tuple(dst_off)].at[pl.ds(lo, n)],
            asem_s.at[k], asem_r.at[k], plane(*d))
        used[(tuple(dst_off), axis, sign, lo)] = cp

    def await_piece(off, axis, sign, lo):
        used[(off, axis, sign, lo)].wait_recv()

    def off(axis, a, b):
        return (a, b) if axis == 0 else (b, a)

    lax.fori_loop(0, HALF, pack, 0)
    pl.semaphore_wait(barrier, len(others))

    def spread(h, axis, o):
        apiece(o, axis, 1, h * HALF, HALF)
        apiece(o, axis, -1, h * HALF, HALF)

    def got(h, axis, o1, o3):
        await_piece(o3, axis, 1, h * HALF)
        apiece(o3, axis, 1, h * HALF, QUART)
        await_piece(o1, axis, -1, h * HALF)
        apiece(o1, axis, -1, h * HALF + QUART, QUART)

    def far(h, axis, o2):
        await_piece(o2, axis, 1, h * HALF)
        await_piece(o2, axis, -1, h * HALF + QUART)

    def mcopy(k, lo, n, to, dev):
        return remote(meta.at[pl.ds(lo, n)], meta.at[pl.ds(to, n)], msem_s.at[k], msem_r.at[k], dev)

    m_x = [mcopy(0, 0, 1, 3, plane(1, 0)), mcopy(1, 0, 1, 1, plane(3, 0))]

    spread(0, 0, (0, 0))
    lax.fori_loop(HALF, SLOTS, pack, 0)
    spread(1, 1, (0, 0))
    def own_panel(r, carry):
        for c in range(PT):
            ball[pl.ds(row * ROWS + r * T, T), c * T:(c + 1) * T] = own[meta_s[0, c, r]]
        return carry

    lax.fori_loop(0, RT, own_panel, 0)

    def bcopy(k, dy_src, core_src, lo, n, dev):
        blk = ball.at[pl.ds((((y + dy_src) % 4) * 2 + core_src) * ROWS + lo, n)]
        return remote(blk, blk, bsem_s.at[k], bsem_r.at[k], dev)

    HB = ROWS // 2
    b_up = bcopy(0, 0, core, 0, ROWS, line(1, 0))
    b_dn = bcopy(1, 0, core, 0, ROWS, line(-1, 0))
    b_sib = [bcopy(2, 0, core, 0, ROWS, line(0, 1))]
    for h in range(2):
        spread(h, 1 - h, (0, 0))
    for cp in m_x:
        cp.wait_recv()
    m_x2 = mcopy(2, 3, 1, 2, plane(1, 0))
    for h in range(2):
        got(h, h, off(h, 1, 0), off(h, 3, 0))
    m_x2.wait_recv()
    m_z = [mcopy(3, 0, 4, 12, plane(0, 1)), mcopy(4, 0, 4, 4, plane(0, 3))]
    for h in range(2):
        spread(h, 1 - h, off(h, 1, 0))
        spread(h, 1 - h, off(h, 3, 0))
    b_up.wait_recv()
    b_up2 = bcopy(3, 3, core, 0, HB, line(1, 0))
    b_sib.append(bcopy(4, 3, core, 0, ROWS, line(0, 1)))
    b_dn.wait_recv()
    b_dn2 = bcopy(5, 1, core, HB, HB, line(-1, 0))
    b_sib.append(bcopy(6, 1, core, 0, ROWS, line(0, 1)))
    for h in range(2):
        far(h, h, off(h, 2, 0))
    for h in range(2):
        got(h, 1 - h, off(h, 0, 1), off(h, 0, 3))
    for h in range(2):
        spread(h, 1 - h, off(h, 2, 0))
    for cp in m_z:
        cp.wait_recv()
    m_z2 = mcopy(5, 12, 4, 8, plane(0, 1))

    def fetch_maps(lo):
        cp = pltpu.make_async_copy(meta.at[pl.ds(lo, 4)], meta_s.at[pl.ds(lo, 4)], loc_sem.at[KT])
        cp.start()
        cp.wait()

    for lo in (0, 4, 12):
        fetch_maps(lo)
    b_up2.wait_recv()
    b_sib.append(bcopy(7, 2, core, 0, HB, line(0, 1)))
    b_dn2.wait_recv()
    b_sib.append(bcopy(8, 2, core, HB, HB, line(0, 1)))
    for cp in b_sib:
        cp.wait_recv()

    first = [True]

    def multiply(o):
        buf, m = bufs[o], o[1] * 4 + o[0]
        zero = first[0]
        first[0] = False
        src = ((x + o[0]) % 4) * 4 + (z + o[1]) % 4

        for r in range(RT):
            for c in range(KT):
                dense[r * T:(r + 1) * T, c * T:(c + 1) * T] = buf[meta_s[m, c, r]]
        p = jnp.dot(dense[...], ball[pl.ds(src * KW, KW), :], preferred_element_type=jnp.float32)
        if zero:
            acc[...] = p
        else:
            acc[...] += p

    for o in ((0, 0), (1, 0), (3, 0), (0, 1), (0, 3)):
        multiply(o)
    for s in (1, 3):
        for h in range(2):
            got(h, 1 - h, off(h, s, 1), off(h, s, 3))
    for h in range(2):
        far(h, 1 - h, off(h, 0, 2))
    m_z2.wait_recv()
    fetch_maps(8)
    for o in ((2, 0), (0, 2), (1, 1)):
        multiply(o)
    for h in range(2):
        got(h, 1 - h, off(h, 2, 1), off(h, 2, 3))
    for o in ((1, 3), (3, 1), (3, 3)):
        multiply(o)
    for s in (1, 3):
        for h in range(2):
            far(h, 1 - h, off(h, s, 2))
        multiply((s, 2))
        multiply((2, s))
    for h in range(2):
        far(h, 1 - h, off(h, 2, 2))
    multiply((2, 2))

    sums = [jnp.zeros((8, T), jnp.float32)] * PT
    sqs = [jnp.zeros((8, T), jnp.float32)] * PT
    mxs = [jnp.zeros((8, T), jnp.float32)] * PT

    def finish(r, carry):
        out = []
        for c in range(PT):
            s, q, m = carry[c]
            sl = (pl.ds(r * T, T), slice(c * T, (c + 1) * T))
            v = acc[sl] * kept_ref[c, r].astype(jnp.float32)
            v = v * v
            acc[sl] = v
            v8 = v.reshape(T // 8, 8, T)
            out.append((s + jnp.sum(v8, axis=0), q + jnp.sum(v8 * v8, axis=0), jnp.maximum(m, jnp.max(v8, axis=0))))
        return tuple(out)

    fin = lax.fori_loop(0, RT, finish, tuple((sums[c], sqs[c], mxs[c]) for c in range(PT)))
    for c in range(PT):
        s, q, m = fin[c]
        stats[row, 0:1, c * T:(c + 1) * T] = jnp.sum(s, axis=0, keepdims=True)
        stats[row, 1:2, c * T:(c + 1) * T] = jnp.sum(q, axis=0, keepdims=True)
        stats[row, 2:3, c * T:(c + 1) * T] = jnp.max(m, axis=0, keepdims=True)
    lines = [(dy, dc) for dy in range(4) for dc in range(2) if (dy, dc) != (0, 0)]
    cps = []
    for i, (dy, dc) in enumerate(lines):
        j = lines.index(((-dy) % 4, dc))
        cps.append(remote(stats.at[row], stats.at[row], ssem_s.at[i], ssem_r.at[j], line(dy, dc)))
    for cp in cps:
        cp.wait_recv()
    col_sums, squares, col_max = stats[0, 0:1, :], stats[0, 1:2, :], stats[0, 2:3, :]
    for i in range(1, 8):
        col_sums = col_sums + stats[i, 0:1, :]
        squares = squares + stats[i, 1:2, :]
        col_max = jnp.maximum(col_max, stats[i, 2:3, :])
    peak = col_max / col_sums - squares / (col_sums * col_sums)
    peak = jnp.maximum(jnp.maximum(peak[:, :T], peak[:, T:2 * T]), peak[:, 2 * T:])
    peaks[0] = jnp.broadcast_to(peak, (8, T))
    cps = []
    for i, o in enumerate(OFFS[1:]):
        j = OFFS[1:].index(((-o[0]) % 4, (-o[1]) % 4))
        cps.append(remote(peaks.at[0], peaks.at[1 + j], csem_s.at[i], csem_r.at[j], plane(*o)))
    inverse = 1.0 / col_sums
    nodes = float(8 * ROWS)
    out_ref[...] = acc[...] * inverse * nodes
    for cp in sends:
        cp.wait_send()
    for cp in cps:
        cp.wait_recv()
    best = peaks[0]
    for i in range(1, 16):
        best = jnp.maximum(best, peaks[i])
    chaos_ref[0, 0] = jnp.max(best) * nodes


def body(transition, tile_pattern, kept_tiles):
    a = transition.reshape(RT, T, KW)
    dma = pltpu.SemaphoreType.DMA
    panel, chaos = pl.pallas_call(
        main_kernel,
        out_shape=(
            jax.ShapeDtypeStruct((ROWS, W), jnp.float32),
            jax.ShapeDtypeStruct((1, 1), jnp.float32),
        ),
        in_specs=[
            pl.BlockSpec(memory_space=pltpu.SMEM),
            pl.BlockSpec(memory_space=pltpu.SMEM),
            pl.BlockSpec(memory_space=pltpu.HBM),
        ],
        out_specs=(
            pl.BlockSpec(memory_space=pltpu.VMEM),
            pl.BlockSpec(memory_space=pltpu.SMEM),
        ),
        scratch_shapes=[pltpu.VMEM((SLOTS + 1, T, T), jnp.bfloat16)] * 16
        + [
            pltpu.VMEM((RT * KT, T, T), jnp.bfloat16),
            pltpu.VMEM((8 * ROWS, W), jnp.bfloat16),
            pltpu.VMEM((ROWS, W), jnp.float32),
            pltpu.VMEM((ROWS, KW), jnp.bfloat16),
            pltpu.VMEM((16, 8, T), jnp.int32),
            pltpu.SMEM((16, 8, T), jnp.int32),
            pltpu.VMEM((8, 8, W), jnp.float32),
            pltpu.VMEM((16, 8, T), jnp.float32),
            dma((KT + 1,)),
            dma((40,)), dma((40,)),
            dma((9,)), dma((9,)),
            dma((6,)), dma((6,)),
            dma((7,)), dma((7,)),
            dma((15,)), dma((15,)),
        ],
        compiler_params=pltpu.CompilerParams(
            collective_id=0, has_side_effects=True, vmem_limit_bytes=50 * 2**20),
        cost_estimate=pl.CostEstimate(flops=14495514624, bytes_accessed=8 * 2**20, transcendentals=0),
    )(*(pltpu.with_memory_space_constraint(v, pltpu.HBM) for v in (tile_pattern.T, kept_tiles.T, a)))
    return panel, chaos.reshape(())


def solution(mesh):
    placed = (P("row", "col"), P("row", "col"), P("row", "col"))
    return jax.shard_map(
        body, mesh=mesh, in_specs=placed, out_specs=(P("row", "col"), P()), check_vma=False
    )
```
